768 devices in a mesh: ctx: 96 (over z, y_hi, core), ch: 8 (over y_lo, x).
Axes of the slice: x: 4, y: 8 (y_hi: 4, y_lo: 2; y = y_hi * 2 + y_lo), z: 12, core: 2. Of those that a mesh axis runs over, the one named last changes fastest.
Arguments:
- features: bfloat16 [3, 24576, 8192], P(None, 'ctx', 'ch'), may hold values from -6 to 6
- short_filter: float32 [3, 7, 8192], P(None, None, 'ch'), may hold values from -4 to 4
- long_filter: float32 [512, 128], P('ch'), may hold values from -0.5 to 0.5
- cotangent: bfloat16 [24576, 8192], P('ctx', 'ch'), may hold values from -15 to 15
Outputs:
- grad_features: bfloat16 [3, 24576, 8192], P(None, 'ctx', 'ch')
- grad_short: float32 [3, 7, 8192], P(None, None, 'ch')
- grad_long: float32 [512, 128], P('ch')
The draws below stay inside these ranges and needn't reach their ends.
All inputs are finite; a program needn't handle non-finite values.
Results may differ from the reference program's by a relative error of at most 0.0057.
Values may be sent and summed in bfloat16 or wider, within the bound.
A program may use at most 128 MiB of HBM per device.

```python
import math
import jax
import jax.numpy as jnp
from jax import lax

D = 8192
GROUP = 16
G = 512
SHORT_TAPS = 7
LONG_TAPS = 128
TOKENS = 24576


def draw_cotangent(key, part):
    scale_key, value_key = jax.random.split(jax.random.fold_in(key, 11))
    scales = jnp.exp(jax.random.uniform(scale_key, (D,), jnp.float32, math.log(0.5), math.log(5.0)))
    values = jax.random.truncated_normal(value_key, -3.0, 3.0, (TOKENS, D), jnp.float32)
    return (values * scales[None, :]).astype(jnp.bfloat16)


def level_of(key, shape, shards, least, top_value):
    loudness = 1.0
    for position, blocks in shards:
        heights = jax.random.uniform(jax.random.fold_in(jax.random.fold_in(key, 6), position), (blocks,), jnp.float32, least / len(shards), top_value / len(shards))
        loudness = loudness * jnp.repeat(jnp.exp(heights), shape[position] // blocks).reshape((-1,) + (1,) * (len(shape) - 1 - position))
    return loudness


def normal_values(stream_key, shape, width, limit, shards=(), kind=jnp.bfloat16):
    loudness = level_of(stream_key, shape, shards, -0.22, 0.18) if shards else 1.0
    drawn = jax.random.normal(stream_key, shape, jnp.float32) * width * loudness
    return jnp.minimum(jnp.maximum(drawn, -limit), limit).astype(kind)


def setup_inputs(seed: int = 0) -> dict:
    key_of = jax.random.split(jax.random.key(seed), 5)
    return {
        "features": normal_values(key_of[0], (3, TOKENS, D), 1.0, 6.0, ((1, 96), (2, 8))),
        "short_filter": normal_values(key_of[1], (3, SHORT_TAPS, D), 0.4, 4.0, ((2, 8),), jnp.float32),
        "long_filter": normal_values(key_of[2], (G, LONG_TAPS), 0.09, 0.5, ((0, 8),), jnp.float32),
        "cotangent": draw_cotangent(jax.random.fold_in(key_of[4], 71), 0),
    }


def short_conv(extended, filt, count):
    taps = filt.shape[0]
    total = jnp.zeros((count, extended.shape[1]), jnp.float32)
    for tap in range(taps):
        start = taps - 1 - tap
        total = total + filt[tap] * extended[start:start + count].astype(jnp.float32)
    return total

def short_adjoint(grad, filt):
    taps = filt.shape[0]
    count = grad.shape[0]
    edge = jnp.zeros((taps - 1, grad.shape[1]), jnp.float32)
    padded = jnp.concatenate([edge, grad, edge], 0)
    total = jnp.zeros((count + taps - 1, grad.shape[1]), jnp.float32)
    for tap in range(taps):
        total = total + filt[tap] * padded[tap:tap + count + taps - 1]
    return total

def filter_grad(grad, extended, taps):
    count = grad.shape[0]
    pieces = []
    for tap in range(taps):
        start = taps - 1 - tap
        pieces.append(lax.optimization_barrier(jnp.sum(grad * extended[start:start + count].astype(jnp.float32), 0)))
    return jnp.stack(pieces)

def toeplitz(long_filter):
    groups, span = long_filter.shape
    rounded = long_filter.astype(jnp.bfloat16).astype(jnp.float32)
    line = jnp.concatenate([jnp.zeros((groups, 1), jnp.float32), rounded[:, ::-1], jnp.zeros((groups, 2 * span - 1), jnp.float32)], 1)
    flat = jnp.tile(line, (1, span))[:, :span * (3 * span - 1)]
    return flat.reshape(groups, span, 3 * span - 1)[:, :, :2 * span]

def windows(z_pad, groups, span):
    count = z_pad.shape[0] // span
    blocks = z_pad.astype(jnp.float32).reshape(count, span, groups, -1)
    return jnp.concatenate([blocks[:-1], blocks[1:]], 1)

def long_forward(z_pad, matrix, groups, span):
    win = windows(z_pad, groups, span)
    out = jnp.einsum('gts,bsgc->btgc', matrix, win, precision=lax.Precision.HIGHEST)
    return out.reshape(-1, z_pad.shape[1])

def long_adjoint(grad_y, matrix, groups, span):
    count = grad_y.shape[0] // span
    blocks = grad_y.astype(jnp.float32).reshape(count, span, groups, -1)
    win = jnp.einsum('gts,btgc->bsgc', matrix, blocks, precision=lax.Precision.HIGHEST)
    zero = jnp.zeros((1,) + win.shape[1:2] + win.shape[2:], jnp.float32)[:, :span]
    total = jnp.concatenate([win[:, :span], zero], 0) + jnp.concatenate([zero, win[:, span:]], 0)
    return total.reshape(-1, grad_y.shape[1])

def long_filter_grad(grad_y, z_pad, groups, span):
    count = grad_y.shape[0] // span
    blocks = grad_y.astype(jnp.float32).reshape(count, span, groups, -1)
    win = windows(z_pad, groups, span)
    inner = jnp.einsum('btgc,bsgc->gts', blocks, win, precision=lax.Precision.HIGHEST)
    inner = jnp.concatenate([inner, jnp.zeros((groups, span, span), jnp.float32)], 2)
    flat = jnp.concatenate([inner.reshape(groups, span * 3 * span), jnp.zeros((groups, span), jnp.float32)], 1)
    skewed = flat.reshape(groups, span, 3 * span + 1)
    columns = lax.optimization_barrier(jnp.sum(skewed, 1))
    return columns[:, 1:span + 1][:, ::-1]

def reference(features, short_filter, long_filter, cotangent):
    taps = SHORT_TAPS
    span = LONG_TAPS
    reach = span + taps - 2
    block = math.gcd(D, 512)
    count = D // block
    groups = block // GROUP

    def one_block(index):
        first = (index * block).astype(jnp.int32)
        feats = lax.dynamic_slice_in_dim(features, first, block, 2)
        filt = lax.dynamic_slice_in_dim(short_filter, first, block, 2)
        longf = lax.dynamic_slice_in_dim(long_filter, (index * groups).astype(jnp.int32), groups, 0)
        cot = lax.dynamic_slice_in_dim(cotangent, first, block, 1).astype(jnp.float32)
        q_ext = jnp.concatenate([jnp.zeros((taps - 1, block), jnp.bfloat16), feats[0]], 0)
        k_ext = jnp.concatenate([jnp.zeros((reach, block), jnp.bfloat16), feats[1]], 0)
        v_ext = jnp.concatenate([jnp.zeros((reach, block), jnp.bfloat16), feats[2]], 0)
        q_short = short_conv(q_ext, filt[0], TOKENS)
        k_short = short_conv(k_ext, filt[1], TOKENS + span - 1)
        v_short = short_conv(v_ext, filt[2], TOKENS + span - 1)
        gated = (k_short * v_short).astype(jnp.bfloat16)
        z_pad = jnp.concatenate([jnp.zeros((1, block), jnp.bfloat16), gated], 0)
        matrix = toeplitz(longf)
        y_long = long_forward(z_pad, matrix, groups, span)
        grad_y = (cot * q_short).astype(jnp.bfloat16)
        grad_q_short = cot * y_long
        grad_z = long_adjoint(grad_y, matrix, groups, span)[1:]
        grad_k_short = grad_z * v_short
        grad_v_short = grad_z * k_short
        grad_q = short_adjoint(grad_q_short, filt[0])[taps - 1:]
        grad_k = short_adjoint(grad_k_short, filt[1])[reach:]
        grad_v = short_adjoint(grad_v_short, filt[2])[reach:]
        raw_short = jnp.stack([filter_grad(grad_q_short, q_ext, taps), filter_grad(grad_k_short, k_ext, taps), filter_grad(grad_v_short, v_ext, taps)])
        raw_long = long_filter_grad(grad_y, z_pad, groups, span)
        grads = jnp.stack([grad_q, grad_k, grad_v]).astype(jnp.bfloat16)
        return (grads, raw_short, raw_long)
    grads, raw_short, raw_long = lax.map(one_block, jnp.arange(count, dtype=jnp.int32))
    grad_features = grads.transpose(1, 2, 0, 3).reshape(3, TOKENS, D)
    raw_short = raw_short.transpose(1, 2, 0, 3).reshape(3, taps, D)
    raw_long = raw_long.reshape(G, span)
    mean_square = (jnp.sum(raw_short * raw_short) + jnp.sum(raw_long * raw_long)) / (3 * taps * D + span * G)
    factor = lax.rsqrt(mean_square + 1e-06)
    return (grad_features, raw_short * factor, raw_long * factor)
```

```python
import jax
import jax.numpy as jnp
from jax import lax
from jax.experimental import pallas as pl
from jax.experimental.pallas import tpu as pltpu
from jax.sharding import PartitionSpec as P

MESH = pl.DeviceIdType.MESH
F32 = jnp.float32
BF16 = jnp.bfloat16

ROWS = 256
SPAN = 128
LANES = 128
TILES = 8
PLANES = 12
CH = 8
GROUP = 16
PER = LANES // GROUP
TAPS = 7
HEAD = 8
COUNT = 237568


def kernel(
    feat, sf, lf, cot, out_grads, out_short, out_long,
    xf, ks, vs, zw, dyw, fwd, bwd, dd, amat, bmat, hrev, gout,
    rawb, scat, gath, fin, sq,
    fwd_s, fwd_r, bwd_s, bwd_r, dd_s, dd_r, rs_s, rs_r, z_s, z_r, ag_s, ag_r, ch_s, ch_r, out_s,
):
    me = lax.axis_index("ctx")
    mc = lax.axis_index("ch")
    last = PLANES * TILES - 1
    plane = me // TILES
    part = lax.rem(me, TILES)
    after = lax.rem(me + 1, PLANES * TILES)
    before = lax.rem(me + last, PLANES * TILES)

    def z_peer(d):
        return lax.rem(plane + d, PLANES)

    def p_peer(d):
        return lax.rem(part + d, TILES)

    def c_peer(d):
        return lax.rem(mc + d, CH)

    barrier = pltpu.get_barrier_semaphore()
    peers = [(before, mc), (after, mc)]
    peers += [(plane * TILES + p_peer(d), mc) for d in range(1, TILES)]
    peers += [(me, c_peer(d)) for d in range(1, CH)]
    peers += [(z_peer(d) * TILES + part, mc) for d in range(1, PLANES)]
    for peer in peers:
        pl.semaphore_signal(barrier, inc=1, device_id=peer, device_id_type=MESH)

    def lanes(tile):
        return pl.ds(pl.multiple_of(tile * LANES, LANES), LANES)

    def taps(which, tile, start, count):
        total = sf[which, 0:1, lanes(tile)] * xf[tile, which, pl.ds(HEAD + start, count), :]
        for j in range(1, TAPS):
            total += sf[which, j : j + 1, lanes(tile)] * xf[tile, which, pl.ds(HEAD + start - j, count), :]
        return total

    def remote(src, dst, send, recv, ctx, ch):
        return pltpu.make_async_remote_copy(
            src_ref=src, dst_ref=dst, send_sem=send, recv_sem=recv, device_id=(ctx, ch), device_id_type=MESH
        )

    def fwd_copy(tile):
        return remote(fwd.at[tile], zw.at[tile, pl.ds(0, 160)], fwd_s.at[tile], fwd_r.at[tile], after, mc)

    def bwd_copy(tile):
        return remote(bwd.at[tile], dyw.at[tile, pl.ds(ROWS, 144)], bwd_s.at[tile], bwd_r.at[tile], before, mc)

    def dd_copy(tile):
        return remote(
            dd.at[tile, :, pl.ds(0, 8)], dd.at[tile, :, pl.ds(ROWS, 8)], dd_s.at[tile], dd_r.at[tile], before, mc
        )

    def first(tile, _):
        zero8 = jnp.zeros((8, LANES), F32)
        for which in range(3):
            xf[tile, which, pl.ds(HEAD, ROWS), :] = feat[which, :, lanes(tile)].astype(F32)
        k_short = taps(1, tile, 8, ROWS - 8)
        ks[tile, pl.ds(8, ROWS - 8), :] = k_short
        v_short = taps(2, tile, 8, ROWS - 8)
        vs[tile, pl.ds(8, ROWS - 8), :] = v_short
        gated = jnp.concatenate([zero8, k_short * v_short], 0).astype(BF16)
        zw[tile, pl.ds(160, ROWS), :] = gated
        tails = [xf[tile, which, pl.ds(ROWS, 8), :] for which in range(3)] + [zero8]
        fwd[tile, pl.ds(0, 32), :] = jnp.concatenate(tails, 0).astype(BF16)
        fwd[tile, pl.ds(32, SPAN), :] = gated[SPAN:]

        cotf = cot[:, lanes(tile)].astype(F32)
        grad_y = jnp.concatenate([zero8, cotf[8:] * taps(0, tile, 8, ROWS - 8)], 0).astype(BF16)
        dyw[tile, pl.ds(0, ROWS), :] = grad_y
        bwd[tile, pl.ds(0, SPAN), :] = grad_y[:SPAN]
        bwd[tile, pl.ds(SPAN, 16), :] = jnp.concatenate(
            [xf[tile, 0, pl.ds(HEAD, 8), :], cotf[:8]], 0
        ).astype(BF16)

        @pl.when(tile == 0)
        def _():
            pl.semaphore_wait(barrier, len(peers))

        fwd_copy(tile).start()
        bwd_copy(tile).start()
        return 0

    lax.fori_loop(0, TILES, first, 0)

    row = lax.broadcasted_iota(jnp.int32, (SPAN, SPAN), 0)
    col = lax.broadcasted_iota(jnp.int32, (SPAN, SPAN), 1)
    flip = jnp.where(row + col == SPAN - 1, 1.0, 0.0).astype(BF16)
    hb = lf[...].astype(BF16)
    hrev[0] = hb.astype(F32)
    hrev[1] = jnp.dot(hb, flip, preferred_element_type=F32)

    def build(g, _):
        wide = [
            jnp.broadcast_to(
                jnp.concatenate([hrev[i, pl.ds(g, 1), :], jnp.zeros((1, SPAN), F32)], 1), (SPAN, 2 * SPAN)
            )
            for i in range(2)
        ]
        bmat[g] = pltpu.roll(wide[0], 0, axis=1, stride=1, stride_axis=0).astype(BF16)
        amat[g] = pltpu.roll(wide[1], 1, axis=1, stride=1, stride_axis=0).astype(BF16)
        return 0

    lax.fori_loop(0, TILES * PER, build, 0)

    lane = lax.rem(lax.broadcasted_iota(jnp.int32, (1, 2 * LANES), 1), LANES) // GROUP

    def pick(stacked):
        total = stacked[:SPAN]
        for g in range(1, PER):
            total = jnp.where(lane == g, stacked[g * SPAN : (g + 1) * SPAN], total)
        return total[:, :LANES], total[:, LANES:]

    def second(tile, _):
        fwd_copy(tile).wait_recv()
        bwd_copy(tile).wait_recv()

        @pl.when(me == 0)
        def _():
            zw[tile, pl.ds(0, 160), :] = jnp.zeros((160, LANES), BF16)

        @pl.when(me == last)
        def _():
            dyw[tile, pl.ds(ROWS, 144), :] = jnp.zeros((144, LANES), BF16)

        halo = zw[tile, pl.ds(0, 32), :].astype(F32)
        for which in range(3):
            xf[tile, which, pl.ds(0, HEAD), :] = halo[8 * which : 8 * which + 8]
        ahead = dyw[tile, pl.ds(ROWS + SPAN, 16), :].astype(F32)
        xf[tile, 0, pl.ds(HEAD + ROWS, 8), :] = ahead[:8]
        k_head = taps(1, tile, 0, 8)
        v_head = taps(2, tile, 0, 8)
        ks[tile, pl.ds(0, 8), :] = k_head
        vs[tile, pl.ds(0, 8), :] = v_head

        def patch(ref, start, value):
            old = ref[tile, pl.ds(start, 16), :].astype(F32)
            ref[tile, pl.ds(start, 16), :] = jnp.concatenate([value, old[8:]], 0).astype(BF16)

        cotf = cot[:, lanes(tile)].astype(F32)
        patch(zw, 160, k_head * v_head)
        patch(dyw, 0, cotf[:8] * taps(0, tile, 0, 8))
        patch(dyw, ROWS, ahead[8:] * taps(0, tile, ROWS, 8))

        z_win = jnp.concatenate([zw[tile, pl.ds(32, 256), :], zw[tile, pl.ds(160, 256), :]], 1)
        d_win = jnp.concatenate([dyw[tile, pl.ds(0, 256), :], dyw[tile, pl.ds(128, 256), :]], 1)
        groups = pl.ds(tile * PER, PER)
        y_all = jnp.dot(amat[groups].reshape(PER * SPAN, 2 * SPAN), z_win, preferred_element_type=F32)
        y0, y1 = pick(y_all)
        dd[tile, 0, pl.ds(0, SPAN), :] = cotf[:SPAN] * y0
        dd[tile, 0, pl.ds(SPAN, SPAN), :] = cotf[SPAN:] * y1
        g_all = jnp.dot(bmat[groups].reshape(PER * SPAN, 2 * SPAN), d_win, preferred_element_type=F32)
        for b, gz in enumerate(pick(g_all)):
            at = pl.ds(b * SPAN, SPAN)
            dd[tile, 1, at, :] = gz * vs[tile, at, :]
            dd[tile, 2, at, :] = gz * ks[tile, at, :]
        dd_copy(tile).start()

        z_own = jnp.concatenate([zw[tile, pl.ds(160, SPAN), :], zw[tile, pl.ds(160 + SPAN, SPAN), :]], 1)
        z_own = jnp.dot(flip, z_own, preferred_element_type=F32).astype(BF16)
        masked = jnp.concatenate([z_own * (lane == g).astype(BF16) for g in range(PER)], 0)
        gram = lax.dot_general(masked, d_win, (((1,), (1,)), ((), ())), preferred_element_type=F32)
        for g in range(PER):
            skew = pltpu.roll(
                gram[g * SPAN : (g + 1) * SPAN], SPAN + 1, axis=1, stride=1, stride_axis=0
            )
            rawb[tile, 24 + g : 25 + g, :] = jnp.sum(skew[:, :SPAN], 0, keepdims=True)
        for which in range(3):
            for j in range(TAPS):
                prod = dd[tile, which, pl.ds(0, ROWS), :] * xf[tile, which, pl.ds(HEAD - j, ROWS), :]
                rawb[tile, 8 * which + j : 8 * which + j + 1, :] = jnp.sum(prod, 0, keepdims=True)
            rawb[tile, 8 * which + 7 : 8 * which + 8, :] = jnp.zeros((1, LANES), F32)

        @pl.when(tile != part)
        def _():
            remote(
                rawb.at[tile], scat.at[part], rs_s.at[tile], rs_r.at[part], plane * TILES + tile, mc
            ).start()

        @pl.when(tile == part)
        def _():
            scat[part] = rawb[tile]

        return 0

    lax.fori_loop(0, TILES, second, 0)

    def out_copy(tile):
        return pltpu.make_async_copy(
            gout.at[:, :, lanes(tile)], out_grads.at[:, :, lanes(tile)], out_s.at[tile]
        )

    def adjoint(tile, _):
        dd_copy(tile).wait_recv()

        @pl.when(me == last)
        def _():
            dd[tile, :, pl.ds(ROWS, 8), :] = jnp.zeros((3, 8, LANES), F32)

        for which in range(3):
            total = sf[which, 0:1, lanes(tile)] * dd[tile, which, pl.ds(0, ROWS), :]
            for j in range(1, TAPS):
                total += sf[which, j : j + 1, lanes(tile)] * dd[tile, which, pl.ds(j, ROWS), :]
            gout[which, :, lanes(tile)] = total.astype(BF16)
        out_copy(tile).start()
        return 0

    lax.fori_loop(0, 3, adjoint, 0)

    def scat_wait(d, _):
        peer = p_peer(d)
        remote(rawb.at[peer], scat.at[peer], rs_s.at[peer], rs_r.at[peer], plane * TILES + peer, mc).wait()
        return 0

    lax.fori_loop(1, TILES, scat_wait, 0)
    gath[plane] = jnp.sum(scat[...], 0)

    def z_copy(peer, slot):
        return remote(
            gath.at[plane], gath.at[slot], z_s.at[peer], z_r.at[slot], peer * TILES + part, mc
        )

    def z_start(d, _):
        z_copy(z_peer(d), plane).start()
        return 0

    def z_wait(d, _):
        z_copy(z_peer(d), z_peer(d)).wait()
        return 0

    lax.fori_loop(1, PLANES, z_start, 0)
    lax.fori_loop(3, TILES, adjoint, 0)
    lax.fori_loop(1, PLANES, z_wait, 0)
    fin[part] = jnp.sum(gath[...], 0)

    def ag_copy(peer, slot):
        return remote(fin.at[part], fin.at[slot], ag_s.at[peer], ag_r.at[slot], plane * TILES + peer, mc)

    def ag_start(d, _):
        ag_copy(p_peer(d), part).start()
        return 0

    def ag_wait(d, _):
        ag_copy(p_peer(d), p_peer(d)).wait()
        return 0

    lax.fori_loop(1, TILES, ag_start, 0)
    lax.fori_loop(1, TILES, ag_wait, 0)
    whole = fin[...].reshape(TILES * 32 // 8, 8, LANES)
    sq[mc] = jnp.sum(whole * whole, 0)

    def ch_copy(peer, slot):
        return remote(sq.at[mc], sq.at[slot], ch_s.at[peer], ch_r.at[slot], me, peer)

    def ch_start(d, _):
        ch_copy(c_peer(d), mc).start()
        return 0

    def ch_wait(d, _):
        ch_copy(c_peer(d), c_peer(d)).wait()
        return 0

    lax.fori_loop(1, CH, ch_start, 0)
    lax.fori_loop(1, CH, ch_wait, 0)
    total = jnp.sum(sq[...], 0)
    total = jnp.sum(jnp.sum(total, 0, keepdims=True), 1, keepdims=True)
    factor = lax.rsqrt(total / COUNT + 1e-06)
    for tile in range(TILES):
        for which in range(3):
            out_short[which, :, tile * LANES : (tile + 1) * LANES] = (
                fin[tile, 8 * which : 8 * which + TAPS, :] * factor
            )
        out_long[8 * tile : 8 * tile + 8, :] = fin[tile, 24:32, :] * factor

    def drain(tile, _):
        fwd_copy(tile).wait_send()
        bwd_copy(tile).wait_send()
        dd_copy(tile).wait_send()
        out_copy(tile).wait()
        return 0

    lax.fori_loop(0, TILES, drain, 0)


def on_device(features, short_filter, long_filter, cotangent):
    vmem = pl.BlockSpec(memory_space=pltpu.VMEM)
    sems = [pltpu.SemaphoreType.DMA((n,)) for n in (8,) * 8 + (12, 12) + (8,) * 5]
    return pl.pallas_call(
        kernel,
        out_shape=(
            jax.ShapeDtypeStruct((3, ROWS, TILES * LANES), BF16),
            jax.ShapeDtypeStruct((3, TAPS, TILES * LANES), F32),
            jax.ShapeDtypeStruct((TILES * PER, SPAN), F32),
        ),
        in_specs=[vmem] * 4,
        out_specs=(pl.BlockSpec(memory_space=pl.ANY), vmem, vmem),
        scratch_shapes=[
            pltpu.VMEM((TILES, 3, HEAD + ROWS + 8, LANES), F32),
            pltpu.VMEM((TILES, ROWS, LANES), F32),
            pltpu.VMEM((TILES, ROWS, LANES), F32),
            pltpu.VMEM((TILES, 416, LANES), BF16),
            pltpu.VMEM((TILES, 400, LANES), BF16),
            pltpu.VMEM((TILES, 160, LANES), BF16),
            pltpu.VMEM((TILES, 144, LANES), BF16),
            pltpu.VMEM((TILES, 3, ROWS + 8, LANES), F32),
            pltpu.VMEM((TILES * PER, SPAN, 2 * SPAN), BF16),
            pltpu.VMEM((TILES * PER, SPAN, 2 * SPAN), BF16),
            pltpu.VMEM((2, TILES * PER, SPAN), F32),
            pltpu.VMEM((3, ROWS, TILES * LANES), BF16),
            pltpu.VMEM((TILES, 32, LANES), F32),
            pltpu.VMEM((TILES, 32, LANES), F32),
            pltpu.VMEM((PLANES, 32, LANES), F32),
            pltpu.VMEM((TILES, 32, LANES), F32),
            pltpu.VMEM((CH, 8, LANES), F32),
            *sems,
        ],
        compiler_params=pltpu.CompilerParams(
            collective_id=0, has_side_effects=True, vmem_limit_bytes=48 * 1024 * 1024
        ),
    )(features, short_filter, long_filter, cotangent)


def solution(mesh):
    in_specs = (P(None, "ctx", "ch"), P(None, None, "ch"), P("ch", None), P("ctx", "ch"))
    out_specs = (P(None, "ctx", "ch"), P(None, None, "ch"), P("ch", None))
    return jax.shard_map(
        on_device, mesh=mesh, in_specs=in_specs, out_specs=out_specs, check_vma=False
    )
```

```python
import jax
import jax.numpy as jnp
from jax import lax
from jax.experimental import pallas as pl
from jax.experimental.pallas import tpu as pltpu
from jax.sharding import PartitionSpec as P

MESH = pl.DeviceIdType.MESH
F32 = jnp.float32
BF16 = jnp.bfloat16

ROWS = 256
SPAN = 128
LANES = 128
TILES = 8
PLANES = 12
PAIRS = 6
MEMBERS = 16
CH = 8
GROUP = 16
PER = LANES // GROUP
TAPS = 7
HEAD = 8
COUNT = 237568


def kernel(
    feat_in, sf_in, lf_in, cot_in, out_grads, out_short, out_long,
    feat, sf, lf, cot, xf, ks, vs, zw, dyw, fwd, bwd, dd, amat, bmat, hrev, gout,
    rawb, scat, gath, fin, sq, part_sq,
    fwd_s, fwd_r, bwd_s, bwd_r, dd_s, dd_r, rs_s, rs_r, z_s, z_r, ag_s, ag_r, ch_s, ch_r, sq_s, sq_r, out_s, in_s,
):
    me = lax.axis_index("ctx")
    mc = lax.axis_index("ch")
    last = PLANES * TILES - 1
    plane = me // TILES
    part = lax.rem(me, TILES)
    after = lax.rem(me + 1, PLANES * TILES)
    before = lax.rem(me + last, PLANES * TILES)

    pair = plane // 2
    odd = lax.rem(plane, 2)
    member = odd * TILES + part

    def z_peer(d):
        return lax.rem(pair + d, PAIRS)

    def p_peer(d):
        return lax.rem(member + d, MEMBERS)

    def c_peer(d):
        return lax.rem(mc + d, CH)

    def lanes(tile):
        return pl.ds(pl.multiple_of(tile * LANES, LANES), LANES)

    def feat_copy(tile):
        return pltpu.make_async_copy(feat_in.at[:, :, lanes(tile)], feat.at[:, :, lanes(tile)], in_s.at[tile])

    def cot_copy(tile):
        return pltpu.make_async_copy(cot_in.at[:, lanes(tile)], cot.at[:, lanes(tile)], in_s.at[TILES + tile])

    sf_copy = pltpu.make_async_copy(sf_in, sf, in_s.at[2 * TILES])
    lf_copy = pltpu.make_async_copy(lf_in, lf, in_s.at[2 * TILES + 1])
    sf_copy.start()
    for tile in range(TILES):
        feat_copy(tile).start()
        cot_copy(tile).start()
    lf_copy.start()

    barrier = pltpu.get_barrier_semaphore()
    peers = [(before, mc), (after, mc)]
    peers += [(z_peer(d) * MEMBERS + member, mc) for d in range(1, PAIRS)]
    peers += [(pair * MEMBERS + p_peer(d), mc) for d in range(1, MEMBERS)]
    peers += [(me, c_peer(d)) for d in range(1, CH)]
    for peer in peers:
        pl.semaphore_signal(barrier, inc=1, device_id=peer, device_id_type=MESH)

    def taps(which, tile, start, count):
        total = sf[which, 0:1, lanes(tile)] * xf[tile, which, pl.ds(HEAD + start, count), :]
        for j in range(1, TAPS):
            total += sf[which, j : j + 1, lanes(tile)] * xf[tile, which, pl.ds(HEAD + start - j, count), :]
        return total

    def remote(src, dst, send, recv, ctx, ch):
        return pltpu.make_async_remote_copy(
            src_ref=src, dst_ref=dst, send_sem=send, recv_sem=recv, device_id=(ctx, ch), device_id_type=MESH
        )

    def fwd_copy(tile):
        return remote(fwd.at[tile], zw.at[tile, pl.ds(0, 160)], fwd_s.at[tile], fwd_r.at[tile], after, mc)

    def bwd_copy(tile):
        return remote(bwd.at[tile], dyw.at[tile, pl.ds(ROWS, 144)], bwd_s.at[tile], bwd_r.at[tile], before, mc)

    def dd_copy(tile):
        return remote(
            dd.at[tile, :, pl.ds(0, 8)], dd.at[tile, :, pl.ds(ROWS, 8)], dd_s.at[tile], dd_r.at[tile], before, mc
        )

    def first(tile, _):
        feat_copy(tile).wait()
        cot_copy(tile).wait()
        zero8 = jnp.zeros((8, LANES), F32)
        for which in range(3):
            xf[tile, which, pl.ds(HEAD, ROWS), :] = feat[which, :, lanes(tile)].astype(F32)
        k_short = taps(1, tile, 8, ROWS - 8)
        ks[tile, pl.ds(8, ROWS - 8), :] = k_short
        v_short = taps(2, tile, 8, ROWS - 8)
        vs[tile, pl.ds(8, ROWS - 8), :] = v_short
        gated = jnp.concatenate([zero8, k_short * v_short], 0).astype(BF16)
        zw[tile, pl.ds(160, ROWS), :] = gated
        tails = [xf[tile, which, pl.ds(ROWS, 8), :] for which in range(3)] + [zero8]
        fwd[tile, pl.ds(0, 32), :] = jnp.concatenate(tails, 0).astype(BF16)
        fwd[tile, pl.ds(32, SPAN), :] = gated[SPAN:]

        cotf = cot[:, lanes(tile)].astype(F32)
        grad_y = jnp.concatenate([zero8, cotf[8:] * taps(0, tile, 8, ROWS - 8)], 0).astype(BF16)
        dyw[tile, pl.ds(0, ROWS), :] = grad_y
        bwd[tile, pl.ds(0, SPAN), :] = grad_y[:SPAN]
        bwd[tile, pl.ds(SPAN, 16), :] = jnp.concatenate(
            [xf[tile, 0, pl.ds(HEAD, 8), :], cotf[:8]], 0
        ).astype(BF16)
        return 0

    def send(tile, _):
        fwd_copy(tile).start()
        bwd_copy(tile).start()
        return 0

    sf_copy.wait()
    lax.fori_loop(0, TILES, first, 0)
    pl.semaphore_wait(barrier, len(peers))
    lax.fori_loop(0, TILES, send, 0)
    lf_copy.wait()

    row = lax.broadcasted_iota(jnp.int32, (SPAN, SPAN), 0)
    col = lax.broadcasted_iota(jnp.int32, (SPAN, SPAN), 1)
    flip = jnp.where(row + col == SPAN - 1, 1.0, 0.0).astype(BF16)
    hb = lf[...].astype(BF16)
    hrev[0] = hb.astype(F32)
    hrev[1] = jnp.dot(hb, flip, preferred_element_type=F32)

    def build(g, _):
        wide = [jnp.broadcast_to(hrev[i, pl.ds(g, 1), :], (SPAN, SPAN)) for i in range(2)]
        ahead = pltpu.roll(wide[0], 0, axis=1, stride=1, stride_axis=0)
        behind = pltpu.roll(wide[1], 1, axis=1, stride=1, stride_axis=0)
        bmat[g, :, :SPAN] = jnp.where(col >= row, ahead, 0.0).astype(BF16)
        bmat[g, :, SPAN:] = jnp.where(col < row, ahead, 0.0).astype(BF16)
        amat[g, :, :SPAN] = jnp.where(col > row, behind, 0.0).astype(BF16)
        amat[g, :, SPAN:] = jnp.where(col <= row, behind, 0.0).astype(BF16)
        return 0

    lax.fori_loop(0, TILES * PER, build, 0, unroll=4)

    lane = lax.rem(lax.broadcasted_iota(jnp.int32, (1, 2 * LANES), 1), LANES) // GROUP

    def pick(stacked):
        total = stacked[:SPAN]
        for g in range(1, PER):
            total = jnp.where(lane == g, stacked[g * SPAN : (g + 1) * SPAN], total)
        return total[:, :LANES], total[:, LANES:]

    def scat_copy(owner, slot):
        return remote(
            rawb.at[owner], scat.at[slot], rs_s.at[owner], rs_r.at[slot], pair * MEMBERS + owner, mc
        )

    def second(tile, _):
        fwd_copy(tile).wait_recv()
        bwd_copy(tile).wait_recv()

        @pl.when(me == 0)
        def _():
            zw[tile, pl.ds(0, 160), :] = jnp.zeros((160, LANES), BF16)

        @pl.when(me == last)
        def _():
            dyw[tile, pl.ds(ROWS, 144), :] = jnp.zeros((144, LANES), BF16)

        halo = zw[tile, pl.ds(0, 32), :].astype(F32)
        for which in range(3):
            xf[tile, which, pl.ds(0, HEAD), :] = halo[8 * which : 8 * which + 8]
        ahead = dyw[tile, pl.ds(ROWS + SPAN, 16), :].astype(F32)
        xf[tile, 0, pl.ds(HEAD + ROWS, 8), :] = ahead[:8]
        k_head = taps(1, tile, 0, 8)
        v_head = taps(2, tile, 0, 8)
        ks[tile, pl.ds(0, 8), :] = k_head
        vs[tile, pl.ds(0, 8), :] = v_head

        def patch(ref, start, value):
            old = ref[tile, pl.ds(start, 16), :].astype(F32)
            ref[tile, pl.ds(start, 16), :] = jnp.concatenate([value, old[8:]], 0).astype(BF16)

        cotf = cot[:, lanes(tile)].astype(F32)
        patch(zw, 160, k_head * v_head)
        patch(dyw, 0, cotf[:8] * taps(0, tile, 0, 8))
        patch(dyw, ROWS, ahead[8:] * taps(0, tile, ROWS, 8))

        z_win = jnp.concatenate([zw[tile, pl.ds(32, 256), :], zw[tile, pl.ds(160, 256), :]], 1)
        d_win = jnp.concatenate([dyw[tile, pl.ds(0, 256), :], dyw[tile, pl.ds(128, 256), :]], 1)
        groups = pl.ds(tile * PER, PER)
        y_all = jnp.dot(amat[groups].reshape(PER * SPAN, 2 * SPAN), z_win, preferred_element_type=F32)
        y0, y1 = pick(y_all)
        dd[tile, 0, pl.ds(0, SPAN), :] = cotf[:SPAN] * y0
        dd[tile, 0, pl.ds(SPAN, SPAN), :] = cotf[SPAN:] * y1
        g_all = jnp.dot(bmat[groups].reshape(PER * SPAN, 2 * SPAN), d_win, preferred_element_type=F32)
        for b, gz in enumerate(pick(g_all)):
            at = pl.ds(b * SPAN, SPAN)
            dd[tile, 1, at, :] = gz * vs[tile, at, :]
            dd[tile, 2, at, :] = gz * ks[tile, at, :]
        dd_copy(tile).start()

        z_own = jnp.concatenate([zw[tile, pl.ds(160, SPAN), :], zw[tile, pl.ds(160 + SPAN, SPAN), :]], 1)
        z_own = jnp.dot(flip, z_own, preferred_element_type=F32).astype(BF16)
        masked = jnp.concatenate([z_own * (lane == g).astype(BF16) for g in range(PER)], 0)
        gram = lax.dot_general(masked, d_win, (((1,), (1,)), ((), ())), preferred_element_type=F32)
        for g in range(PER):
            rows = gram[g * SPAN : (g + 1) * SPAN]
            both = jnp.where(row + col >= SPAN - 1, rows[:, :SPAN], rows[:, SPAN:])
            skew = pltpu.roll(both, 1, axis=1, stride=1, stride_axis=0)
            rawb[TILES + tile, 8 + g : 9 + g, :] = jnp.sum(skew, 0, keepdims=True)
        for which in range(3):
            at, row0 = which // 2 * TILES + tile, which % 2 * 8
            for j in range(TAPS):
                prod = dd[tile, which, pl.ds(0, ROWS), :] * xf[tile, which, pl.ds(HEAD - j, ROWS), :]
                rawb[at, row0 + j : row0 + j + 1, :] = jnp.sum(prod, 0, keepdims=True)
            rawb[at, row0 + 7 : row0 + 8, :] = jnp.zeros((1, LANES), F32)

        for half in range(2):
            owner = half * TILES + tile

            @pl.when(owner != member)
            def _():
                scat_copy(owner, member).start()

            @pl.when(owner == member)
            def _():
                scat[member] = rawb[owner]

        return 0

    lax.fori_loop(0, TILES, second, 0)

    def out_copy(tile):
        return pltpu.make_async_copy(
            gout.at[:, :, lanes(tile)], out_grads.at[:, :, lanes(tile)], out_s.at[tile]
        )

    def adjoint(tile, _):
        dd_copy(tile).wait_recv()

        @pl.when(me == last)
        def _():
            dd[tile, :, pl.ds(ROWS, 8), :] = jnp.zeros((3, 8, LANES), F32)

        for which in range(3):
            total = sf[which, 0:1, lanes(tile)] * dd[tile, which, pl.ds(0, ROWS), :]
            for j in range(1, TAPS):
                total += sf[which, j : j + 1, lanes(tile)] * dd[tile, which, pl.ds(j, ROWS), :]
            gout[which, :, lanes(tile)] = total.astype(BF16)
        out_copy(tile).start()
        return 0

    lax.fori_loop(0, 3, adjoint, 0)

    def scat_wait(d, _):
        scat_copy(p_peer(d), p_peer(d)).wait()
        return 0

    lax.fori_loop(1, MEMBERS, scat_wait, 0)
    gath[pair] = jnp.sum(scat[...], 0)

    def z_copy(peer, slot):
        return remote(
            gath.at[pair], gath.at[slot], z_s.at[peer], z_r.at[slot], peer * MEMBERS + member, mc
        )

    def z_start(d, _):
        z_copy(z_peer(d), pair).start()
        return 0

    def z_wait(d, _):
        z_copy(z_peer(d), z_peer(d)).wait()
        return 0

    lax.fori_loop(1, PAIRS, z_start, 0)
    lax.fori_loop(3, TILES, adjoint, 0)
    lax.fori_loop(1, PAIRS, z_wait, 0)
    fin[member] = jnp.sum(gath[...], 0)

    def ag_copy(peer, slot):
        return remote(fin.at[member], fin.at[slot], ag_s.at[peer], ag_r.at[slot], pair * MEMBERS + peer, mc)

    def ag_start(d, _):
        ag_copy(p_peer(d), member).start()
        return 0

    def ag_wait(d, _):
        ag_copy(p_peer(d), p_peer(d)).wait()
        return 0

    top = pl.ds(0, 1)

    def ch_copy(peer, slot):
        return remote(sq.at[mc, top], sq.at[slot, top], ch_s.at[peer], ch_r.at[slot], me, peer)

    def ch_start(d, _):
        ch_copy(c_peer(d), mc).start()
        return 0

    def ch_wait(d, _):
        ch_copy(c_peer(d), c_peer(d)).wait()
        return 0

    def sq_copy(peer, slot):
        return remote(
            part_sq.at[member, top],
            part_sq.at[slot, top],
            sq_s.at[peer],
            sq_r.at[slot],
            pair * MEMBERS + peer,
            mc,
        )

    def sq_start(d, _):
        sq_copy(p_peer(d), member).start()
        return 0

    def sq_wait(d, _):
        sq_copy(p_peer(d), p_peer(d)).wait()
        return 0

    whole = fin[member]
    sq[mc, top, :] = jnp.sum(whole * whole, 0, keepdims=True)
    lax.fori_loop(1, CH, ch_start, 0)
    lax.fori_loop(1, MEMBERS, ag_start, 0)
    lax.fori_loop(1, CH, ch_wait, 0)
    part_sq[member, top, :] = jnp.sum(sq[:, 0, :], 0, keepdims=True)
    lax.fori_loop(1, MEMBERS, sq_start, 0)
    lax.fori_loop(1, MEMBERS, ag_wait, 0)
    lax.fori_loop(1, MEMBERS, sq_wait, 0)
    total = jnp.sum(jnp.sum(part_sq[:, 0, :], 0, keepdims=True), 1, keepdims=True)
    factor = lax.rsqrt(total / COUNT + 1e-06)
    for tile in range(TILES):
        for which in range(3):
            out_short[which, :, tile * LANES : (tile + 1) * LANES] = (
                fin[which // 2 * TILES + tile, which % 2 * 8 : which % 2 * 8 + TAPS, :] * factor
            )
        out_long[8 * tile : 8 * tile + 8, :] = fin[TILES + tile, 8:16, :] * factor

    def drain(tile, _):
        fwd_copy(tile).wait_send()
        bwd_copy(tile).wait_send()
        dd_copy(tile).wait_send()
        out_copy(tile).wait()
        return 0

    lax.fori_loop(0, TILES, drain, 0)


def on_device(features, short_filter, long_filter, cotangent):
    vmem = pl.BlockSpec(memory_space=pltpu.VMEM)
    hbm = pl.BlockSpec(memory_space=pltpu.HBM)
    sems = [pltpu.SemaphoreType.DMA((n,)) for n in (8,) * 6 + (16, 16, 6, 6, 16, 16, 8, 8, 16, 16, 8, 18)]
    return pl.pallas_call(
        kernel,
        out_shape=(
            jax.ShapeDtypeStruct((3, ROWS, TILES * LANES), BF16),
            jax.ShapeDtypeStruct((3, TAPS, TILES * LANES), F32),
            jax.ShapeDtypeStruct((TILES * PER, SPAN), F32),
        ),
        in_specs=[hbm] * 4,
        out_specs=(pl.BlockSpec(memory_space=pl.ANY), vmem, vmem),
        scratch_shapes=[
            pltpu.VMEM((3, ROWS, TILES * LANES), BF16),
            pltpu.VMEM((3, TAPS, TILES * LANES), F32),
            pltpu.VMEM((TILES * PER, SPAN), F32),
            pltpu.VMEM((ROWS, TILES * LANES), BF16),
            pltpu.VMEM((TILES, 3, HEAD + ROWS + 8, LANES), F32),
            pltpu.VMEM((TILES, ROWS, LANES), F32),
            pltpu.VMEM((TILES, ROWS, LANES), F32),
            pltpu.VMEM((TILES, 416, LANES), BF16),
            pltpu.VMEM((TILES, 400, LANES), BF16),
            pltpu.VMEM((TILES, 160, LANES), BF16),
            pltpu.VMEM((TILES, 144, LANES), BF16),
            pltpu.VMEM((TILES, 3, ROWS + 8, LANES), F32),
            pltpu.VMEM((TILES * PER, SPAN, 2 * SPAN), BF16),
            pltpu.VMEM((TILES * PER, SPAN, 2 * SPAN), BF16),
            pltpu.VMEM((2, TILES * PER, SPAN), F32),
            pltpu.VMEM((3, ROWS, TILES * LANES), BF16),
            pltpu.VMEM((MEMBERS, 16, LANES), F32),
            pltpu.VMEM((MEMBERS, 16, LANES), F32),
            pltpu.VMEM((PAIRS, 16, LANES), F32),
            pltpu.VMEM((MEMBERS, 16, LANES), F32),
            pltpu.VMEM((CH, 8, LANES), F32),
            pltpu.VMEM((MEMBERS, 8, LANES), F32),
            *sems,
        ],
        compiler_params=pltpu.CompilerParams(
            collective_id=0, has_side_effects=True, vmem_limit_bytes=48 * 1024 * 1024
        ),
    )(*(pltpu.with_memory_space_constraint(x, pltpu.HBM) for x in (features, short_filter, long_filter, cotangent)))


def solution(mesh):
    in_specs = (P(None, "ctx", "ch"), P(None, None, "ch"), P("ch", None), P("ctx", "ch"))
    out_specs = (P(None, "ctx", "ch"), P(None, None, "ch"), P("ch", None))
    return jax.shard_map(
        on_device, mesh=mesh, in_specs=in_specs, out_specs=out_specs, check_vma=False
    )
```

```python
import jax
import jax.numpy as jnp
from jax import lax
from jax.experimental import pallas as pl
from jax.experimental.pallas import tpu as pltpu
from jax.sharding import PartitionSpec as P

MESH = pl.DeviceIdType.MESH
F32 = jnp.float32
BF16 = jnp.bfloat16

ROWS = 256
SPAN = 128
LANES = 128
TILES = 8
PLANES = 12
PAIRS = 6
MEMBERS = 16
CH = 8
GROUP = 16
PER = LANES // GROUP
TAPS = 7
HEAD = 8
COUNT = 237568


def kernel(
    feat_in, sf_in, lf_in, cot_in, out_grads, out_short, out_long,
    feat, sf, lf, cot, xf, ks, vs, zw, dyw, fwd, bwd, dd, amat, bmat, hrev, gout,
    rawb, scat, gath, fin, sq, part_sq,
    fwd_s, fwd_r, bwd_s, bwd_r, dd_s, dd_r, rs_s, rs_r, z_s, z_r, ag_s, ag_r, ch_s, ch_r, sq_s, sq_r, out_s, in_s,
):
    me = lax.axis_index("ctx")
    mc = lax.axis_index("ch")
    last = PLANES * TILES - 1
    plane = me // TILES
    part = lax.rem(me, TILES)
    after = lax.rem(me + 1, PLANES * TILES)
    before = lax.rem(me + last, PLANES * TILES)

    pair = plane // 2
    odd = lax.rem(plane, 2)
    member = odd * TILES + part

    def z_peer(d):
        return lax.rem(pair + d, PAIRS)

    def p_peer(d):
        return lax.rem(member + d, MEMBERS)

    def c_peer(d):
        return lax.rem(mc + d, CH)

    def lanes(tile):
        return pl.ds(pl.multiple_of(tile * LANES, LANES), LANES)

    def feat_copy(tile):
        return pltpu.make_async_copy(feat_in.at[:, :, lanes(tile)], feat.at[:, :, lanes(tile)], in_s.at[tile])

    def cot_copy(tile):
        return pltpu.make_async_copy(cot_in.at[:, lanes(tile)], cot.at[:, lanes(tile)], in_s.at[TILES + tile])

    sf_copy = pltpu.make_async_copy(sf_in, sf, in_s.at[2 * TILES])
    lf_copy = pltpu.make_async_copy(lf_in, lf, in_s.at[2 * TILES + 1])
    sf_copy.start()
    for tile in range(TILES):
        feat_copy(tile).start()
        cot_copy(tile).start()
    lf_copy.start()

    barrier = pltpu.get_barrier_semaphore()
    peers = [(before, mc), (after, mc)]
    peers += [(z_peer(d) * MEMBERS + member, mc) for d in range(1, PAIRS)]
    peers += [(pair * MEMBERS + p_peer(d), mc) for d in range(1, MEMBERS)]
    peers += [(me, c_peer(d)) for d in range(1, CH)]
    for peer in peers:
        pl.semaphore_signal(barrier, inc=1, device_id=peer, device_id_type=MESH)

    def taps(which, tile, start, count):
        total = sf[which, 0:1, lanes(tile)] * xf[tile, which, pl.ds(HEAD + start, count), :]
        for j in range(1, TAPS):
            total += sf[which, j : j + 1, lanes(tile)] * xf[tile, which, pl.ds(HEAD + start - j, count), :]
        return total

    def remote(src, dst, send, recv, ctx, ch):
        return pltpu.make_async_remote_copy(
            src_ref=src, dst_ref=dst, send_sem=send, recv_sem=recv, device_id=(ctx, ch), device_id_type=MESH
        )

    def fwd_copy(tile):
        return remote(fwd.at[tile], zw.at[tile, pl.ds(0, 160)], fwd_s.at[tile], fwd_r.at[tile], after, mc)

    def bwd_copy(tile):
        return remote(bwd.at[tile], dyw.at[tile, pl.ds(ROWS, 144)], bwd_s.at[tile], bwd_r.at[tile], before, mc)

    def dd_copy(tile):
        return remote(
            dd.at[tile, :, pl.ds(0, 8)], dd.at[tile, :, pl.ds(ROWS, 8)], dd_s.at[tile], dd_r.at[tile], before, mc
        )

    def first(tile, _):
        feat_copy(tile).wait()
        cot_copy(tile).wait()
        zero8 = jnp.zeros((8, LANES), F32)
        for which in range(3):
            xf[tile, which, pl.ds(HEAD, ROWS), :] = feat[which, :, lanes(tile)].astype(F32)
        k_short = taps(1, tile, 8, ROWS - 8)
        ks[tile, pl.ds(8, ROWS - 8), :] = k_short
        v_short = taps(2, tile, 8, ROWS - 8)
        vs[tile, pl.ds(8, ROWS - 8), :] = v_short
        gated = jnp.concatenate([zero8, k_short * v_short], 0).astype(BF16)
        zw[tile, pl.ds(160, ROWS), :] = gated
        tails = [xf[tile, which, pl.ds(ROWS, 8), :] for which in range(3)] + [zero8]
        fwd[tile, pl.ds(0, 32), :] = jnp.concatenate(tails, 0).astype(BF16)
        fwd[tile, pl.ds(32, SPAN), :] = gated[SPAN:]

        cotf = cot[:, lanes(tile)].astype(F32)
        grad_y = jnp.concatenate([zero8, cotf[8:] * taps(0, tile, 8, ROWS - 8)], 0).astype(BF16)
        dyw[tile, pl.ds(0, ROWS), :] = grad_y
        bwd[tile, pl.ds(0, SPAN), :] = grad_y[:SPAN]
        bwd[tile, pl.ds(SPAN, 16), :] = jnp.concatenate(
            [xf[tile, 0, pl.ds(HEAD, 8), :], cotf[:8]], 0
        ).astype(BF16)
        return 0

    def send(tile, _):
        fwd_copy(tile).start()
        bwd_copy(tile).start()
        return 0

    sf_copy.wait()
    lax.fori_loop(0, TILES, first, 0)
    pl.semaphore_wait(barrier, len(peers))
    lax.fori_loop(0, TILES, send, 0)
    lf_copy.wait()

    row = lax.broadcasted_iota(jnp.int32, (SPAN, SPAN), 0)
    col = lax.broadcasted_iota(jnp.int32, (SPAN, SPAN), 1)
    flip = jnp.where(row + col == SPAN - 1, 1.0, 0.0).astype(BF16)
    hb = lf[...].astype(BF16)
    hrev[0] = hb.astype(F32)
    hrev[1] = jnp.dot(hb, flip, preferred_element_type=F32)

    def build(g, _):
        wide = [jnp.broadcast_to(hrev[i, pl.ds(g, 1), :], (SPAN, SPAN)) for i in range(2)]
        ahead = pltpu.roll(wide[0], 0, axis=1, stride=1, stride_axis=0)
        behind = pltpu.roll(wide[1], 1, axis=1, stride=1, stride_axis=0)
        bmat[g, :, :SPAN] = jnp.where(col >= row, ahead, 0.0).astype(BF16)
        bmat[g, :, SPAN:] = jnp.where(col < row, ahead, 0.0).astype(BF16)
        amat[g, :, :SPAN] = jnp.where(col > row, behind, 0.0).astype(BF16)
        amat[g, :, SPAN:] = jnp.where(col <= row, behind, 0.0).astype(BF16)
        return 0

    lax.fori_loop(0, TILES * PER, build, 0, unroll=4)

    lane = lax.rem(lax.broadcasted_iota(jnp.int32, (1, 2 * LANES), 1), LANES) // GROUP

    def pick(stacked):
        total = stacked[:SPAN]
        for g in range(1, PER):
            total = jnp.where(lane == g, stacked[g * SPAN : (g + 1) * SPAN], total)
        return total[:, :LANES], total[:, LANES:]

    def scat_copy(owner, slot):
        return remote(
            rawb.at[owner], scat.at[slot], rs_s.at[owner], rs_r.at[slot], pair * MEMBERS + owner, mc
        )

    def second(tile, _):
        fwd_copy(tile).wait_recv()
        bwd_copy(tile).wait_recv()

        @pl.when(me == 0)
        def _():
            zw[tile, pl.ds(0, 160), :] = jnp.zeros((160, LANES), BF16)

        @pl.when(me == last)
        def _():
            dyw[tile, pl.ds(ROWS, 144), :] = jnp.zeros((144, LANES), BF16)

        halo = zw[tile, pl.ds(0, 32), :].astype(F32)
        for which in range(3):
            xf[tile, which, pl.ds(0, HEAD), :] = halo[8 * which : 8 * which + 8]
        ahead = dyw[tile, pl.ds(ROWS + SPAN, 16), :].astype(F32)
        xf[tile, 0, pl.ds(HEAD + ROWS, 8), :] = ahead[:8]
        k_head = taps(1, tile, 0, 8)
        v_head = taps(2, tile, 0, 8)
        ks[tile, pl.ds(0, 8), :] = k_head
        vs[tile, pl.ds(0, 8), :] = v_head

        def patch(ref, start, value):
            old = ref[tile, pl.ds(start, 16), :].astype(F32)
            ref[tile, pl.ds(start, 16), :] = jnp.concatenate([value, old[8:]], 0).astype(BF16)

        cotf = cot[:, lanes(tile)].astype(F32)
        patch(zw, 160, k_head * v_head)
        patch(dyw, 0, cotf[:8] * taps(0, tile, 0, 8))
        patch(dyw, ROWS, ahead[8:] * taps(0, tile, ROWS, 8))

        z_win = jnp.concatenate([zw[tile, pl.ds(32, 256), :], zw[tile, pl.ds(160, 256), :]], 1)
        d_win = jnp.concatenate([dyw[tile, pl.ds(0, 256), :], dyw[tile, pl.ds(128, 256), :]], 1)
        groups = pl.ds(tile * PER, PER)
        y_all = jnp.dot(amat[groups].reshape(PER * SPAN, 2 * SPAN), z_win, preferred_element_type=F32)
        y0, y1 = pick(y_all)
        dd[tile, 0, pl.ds(0, SPAN), :] = cotf[:SPAN] * y0
        dd[tile, 0, pl.ds(SPAN, SPAN), :] = cotf[SPAN:] * y1
        g_all = jnp.dot(bmat[groups].reshape(PER * SPAN, 2 * SPAN), d_win, preferred_element_type=F32)
        for b, gz in enumerate(pick(g_all)):
            at = pl.ds(b * SPAN, SPAN)
            dd[tile, 1, at, :] = gz * vs[tile, at, :]
            dd[tile, 2, at, :] = gz * ks[tile, at, :]
        dd_copy(tile).start()

        z_own = jnp.concatenate([zw[tile, pl.ds(160, SPAN), :], zw[tile, pl.ds(160 + SPAN, SPAN), :]], 1)
        z_own = jnp.dot(flip, z_own, preferred_element_type=F32).astype(BF16)
        masked = jnp.concatenate([z_own * (lane == g).astype(BF16) for g in range(PER)], 0)
        gram = lax.dot_general(masked, d_win, (((1,), (1,)), ((), ())), preferred_element_type=F32)
        for g in range(PER):
            rows = gram[g * SPAN : (g + 1) * SPAN]
            both = jnp.where(row + col >= SPAN - 1, rows[:, :SPAN], rows[:, SPAN:])
            skew = pltpu.roll(both, 1, axis=1, stride=1, stride_axis=0)
            rawb[TILES + tile, 8 + g : 9 + g, :] = jnp.sum(skew, 0, keepdims=True)
        for which in range(3):
            at, row0 = which // 2 * TILES + tile, which % 2 * 8
            for j in range(TAPS):
                prod = dd[tile, which, pl.ds(0, ROWS), :] * xf[tile, which, pl.ds(HEAD - j, ROWS), :]
                rawb[at, row0 + j : row0 + j + 1, :] = jnp.sum(prod, 0, keepdims=True)
            rawb[at, row0 + 7 : row0 + 8, :] = jnp.zeros((1, LANES), F32)

        for half in range(2):
            owner = half * TILES + tile

            @pl.when(owner != member)
            def _():
                scat_copy(owner, member).start()

            @pl.when(owner == member)
            def _():
                scat[member] = rawb[owner]

        return 0

    lax.fori_loop(0, TILES, second, 0)

    def out_copy(tile):
        return pltpu.make_async_copy(
            gout.at[:, :, lanes(tile)], out_grads.at[:, :, lanes(tile)], out_s.at[tile]
        )

    def adjoint(tile, _):
        dd_copy(tile).wait_recv()

        @pl.when(me == last)
        def _():
            dd[tile, :, pl.ds(ROWS, 8), :] = jnp.zeros((3, 8, LANES), F32)

        for which in range(3):
            total = sf[which, 0:1, lanes(tile)] * dd[tile, which, pl.ds(0, ROWS), :]
            for j in range(1, TAPS):
                total += sf[which, j : j + 1, lanes(tile)] * dd[tile, which, pl.ds(j, ROWS), :]
            gout[which, :, lanes(tile)] = total.astype(BF16)
        out_copy(tile).start()
        return 0

    lax.fori_loop(0, 3, adjoint, 0)

    def scat_wait(d, _):
        scat_copy(p_peer(d), p_peer(d)).wait()
        return 0

    lax.fori_loop(1, MEMBERS, scat_wait, 0, unroll=True)
    gath[pair] = jnp.sum(scat[...], 0)

    def z_copy(peer, slot):
        return remote(
            gath.at[pair], gath.at[slot], z_s.at[peer], z_r.at[slot], peer * MEMBERS + member, mc
        )

    def z_start(d, _):
        z_copy(z_peer(d), pair).start()
        return 0

    def z_wait(d, _):
        z_copy(z_peer(d), z_peer(d)).wait()
        return 0

    lax.fori_loop(1, PAIRS, z_start, 0, unroll=True)
    lax.fori_loop(3, TILES, adjoint, 0)
    lax.fori_loop(1, PAIRS, z_wait, 0, unroll=True)
    fin[member] = jnp.sum(gath[...], 0)

    def ag_copy(peer, slot):
        return remote(fin.at[member], fin.at[slot], ag_s.at[peer], ag_r.at[slot], pair * MEMBERS + peer, mc)

    def ag_start(d, _):
        ag_copy(p_peer(d), member).start()
        return 0

    def ag_wait(d, _):
        ag_copy(p_peer(d), p_peer(d)).wait()
        return 0

    top = pl.ds(0, 1)

    def ch_copy(peer, slot):
        return remote(sq.at[mc, top], sq.at[slot, top], ch_s.at[peer], ch_r.at[slot], me, peer)

    def ch_start(d, _):
        ch_copy(c_peer(d), mc).start()
        return 0

    def ch_wait(d, _):
        ch_copy(c_peer(d), c_peer(d)).wait()
        return 0

    def sq_copy(peer, slot):
        return remote(
            part_sq.at[member, top],
            part_sq.at[slot, top],
            sq_s.at[peer],
            sq_r.at[slot],
            pair * MEMBERS + peer,
            mc,
        )

    def sq_start(d, _):
        sq_copy(p_peer(d), member).start()
        return 0

    def sq_wait(d, _):
        sq_copy(p_peer(d), p_peer(d)).wait()
        return 0

    whole = fin[member]
    sq[mc, top, :] = jnp.sum(whole * whole, 0, keepdims=True)
    lax.fori_loop(1, CH, ch_start, 0, unroll=True)
    lax.fori_loop(1, MEMBERS, ag_start, 0, unroll=True)
    lax.fori_loop(1, CH, ch_wait, 0, unroll=True)
    part_sq[member, top, :] = jnp.sum(sq[:, 0, :], 0, keepdims=True)
    lax.fori_loop(1, MEMBERS, sq_start, 0, unroll=True)
    lax.fori_loop(1, MEMBERS, ag_wait, 0)
    lax.fori_loop(1, MEMBERS, sq_wait, 0, unroll=True)
    total = jnp.sum(jnp.sum(part_sq[:, 0, :], 0, keepdims=True), 1, keepdims=True)
    factor = lax.rsqrt(total / COUNT + 1e-06)
    for tile in range(TILES):
        for which in range(3):
            out_short[which, :, tile * LANES : (tile + 1) * LANES] = (
                fin[which // 2 * TILES + tile, which % 2 * 8 : which % 2 * 8 + TAPS, :] * factor
            )
        out_long[8 * tile : 8 * tile + 8, :] = fin[TILES + tile, 8:16, :] * factor

    def drain(tile, _):
        fwd_copy(tile).wait_send()
        bwd_copy(tile).wait_send()
        dd_copy(tile).wait_send()
        out_copy(tile).wait()
        return 0

    lax.fori_loop(0, TILES, drain, 0)


def on_device(features, short_filter, long_filter, cotangent):
    vmem = pl.BlockSpec(memory_space=pltpu.VMEM)
    hbm = pl.BlockSpec(memory_space=pltpu.HBM)
    sems = [pltpu.SemaphoreType.DMA((n,)) for n in (8,) * 6 + (16, 16, 6, 6, 16, 16, 8, 8, 16, 16, 8, 18)]
    return pl.pallas_call(
        kernel,
        out_shape=(
            jax.ShapeDtypeStruct((3, ROWS, TILES * LANES), BF16),
            jax.ShapeDtypeStruct((3, TAPS, TILES * LANES), F32),
            jax.ShapeDtypeStruct((TILES * PER, SPAN), F32),
        ),
        in_specs=[hbm] * 4,
        out_specs=(pl.BlockSpec(memory_space=pl.ANY), vmem, vmem),
        scratch_shapes=[
            pltpu.VMEM((3, ROWS, TILES * LANES), BF16),
            pltpu.VMEM((3, TAPS, TILES * LANES), F32),
            pltpu.VMEM((TILES * PER, SPAN), F32),
            pltpu.VMEM((ROWS, TILES * LANES), BF16),
            pltpu.VMEM((TILES, 3, HEAD + ROWS + 8, LANES), F32),
            pltpu.VMEM((TILES, ROWS, LANES), F32),
            pltpu.VMEM((TILES, ROWS, LANES), F32),
            pltpu.VMEM((TILES, 416, LANES), BF16),
            pltpu.VMEM((TILES, 400, LANES), BF16),
            pltpu.VMEM((TILES, 160, LANES), BF16),
            pltpu.VMEM((TILES, 144, LANES), BF16),
            pltpu.VMEM((TILES, 3, ROWS + 8, LANES), F32),
            pltpu.VMEM((TILES * PER, SPAN, 2 * SPAN), BF16),
            pltpu.VMEM((TILES * PER, SPAN, 2 * SPAN), BF16),
            pltpu.VMEM((2, TILES * PER, SPAN), F32),
            pltpu.VMEM((3, ROWS, TILES * LANES), BF16),
            pltpu.VMEM((MEMBERS, 16, LANES), F32),
            pltpu.VMEM((MEMBERS, 16, LANES), F32),
            pltpu.VMEM((PAIRS, 16, LANES), F32),
            pltpu.VMEM((MEMBERS, 16, LANES), F32),
            pltpu.VMEM((CH, 8, LANES), F32),
            pltpu.VMEM((MEMBERS, 8, LANES), F32),
            *sems,
        ],
        compiler_params=pltpu.CompilerParams(
            collective_id=0, has_side_effects=True, vmem_limit_bytes=48 * 1024 * 1024
        ),
    )(*(pltpu.with_memory_space_constraint(x, pltpu.HBM) for x in (features, short_filter, long_filter, cotangent)))


def solution(mesh):
    in_specs = (P(None, "ctx", "ch"), P(None, None, "ch"), P("ch", None), P("ctx", "ch"))
    out_specs = (P(None, "ctx", "ch"), P(None, None, "ch"), P("ch", None))
    return jax.shard_map(
        on_device, mesh=mesh, in_specs=in_specs, out_specs=out_specs, check_vma=False
    )
```
